32 devices in a mesh: groups: 2 (over y), tensor: 8 (over z, x), replica: 2 (over core).
Axes of the slice: x: 2, y: 2, z: 4, core: 2. Of those that a mesh axis runs over, the one named last changes fastest.
Arguments:
- activations: bfloat16 [2, 1024, 8192], P(None, ('groups', 'replica'), 'tensor'), parts along dimension 1, may hold values from -6 to 6
- request_adapter_index: int32 [2, 1024], P(None, 'groups'), parts along dimension 1, may hold values from 0 to 47
- adapter_pool_row: int32 [48], replicated, may hold values from 0 to 47, each once
- gate_weight_matrix: bfloat16 [8192, 28672], P(None, 'tensor'), may hold values from -0.0625 to 0.0625
- adapter_down_factors: bfloat16 [48, 8192, 64], P('replica', 'tensor'), may hold values from -0.0625 to 0.0625
- adapter_up_factors: bfloat16 [48, 64, 28672], P('replica', None, 'tensor'), may hold values from -0.75 to 0.75
Outputs:
- projected: bfloat16 [2, 1024, 28672], P(None, ('groups', 'replica'), 'tensor'), parts along dimension 1
The draws below stay inside these ranges and needn't reach their ends.
There are 2 independent parts, one for each index of `groups`. The reference program is written for one: setup_inputs(seed, part) draws one part's arguments, and reference() takes and returns one part's arrays. A program takes and returns all parts, laid end to end along the dimension named above; an argument that names none is the same for every part. Nothing has to cross between parts.
Inputs may be any that keep to these rules, and one draw needn't show every extreme that they name: `adapter_pool_row`: pool rows r * 24 to (r + 1) * 24 - 1 are those placed on index r of replica; each adapter has one pool row. `request_adapter_index`: each entry names an adapter.
All inputs are finite; a program needn't handle non-finite values.
Results may differ from the reference program's by a relative error of at most 0.0065.
Values may be sent and summed in bfloat16 or wider, within the bound.
A program may use at most 256 MiB of HBM per device.

```python
import math
import jax
import jax.numpy as jnp
import numpy as np
from jax import lax

MODEL_WIDTH = 8192
HIDDEN_UNITS = 28672
ADAPTER_RANK = 64
STEPS = 2
ROWS = 512
ADAPTER_COUNT = 48


def touch_ends(array, own_key, smallest, largest):
    place = [jax.random.randint(jax.random.fold_in(own_key, axis), (), 0, length) for axis, length in enumerate(array.shape)]
    widest = array.shape.index(max(array.shape))
    beside = place[:widest] + [(place[widest] + 1) % array.shape[widest]] + place[widest + 1:]
    return array.at[tuple(place)].set(smallest).at[tuple(beside)].set(largest)


def levels(key, shape, cuts, low, largest):
    level = 1.0
    for position, parts in cuts:
        steps = jax.random.uniform(jax.random.fold_in(jax.random.fold_in(key, 6), position), (parts,), jnp.float32, low / len(cuts), largest / len(cuts))
        level = level * jnp.repeat(jnp.exp(steps), shape[position] // parts).reshape((-1,) + (1,) * (len(shape) - 1 - position))
    return level


def rank_table(count, skew):
    weights = [(1 << 20) // math.isqrt(rank ** skew) + 1 for rank in range(1, count + 1)]
    width = 1 + sum(weights) // (1 << 30)
    return np.cumsum(np.array([max(1, weight // width) for weight in weights]))


def skewed_ids(stream_key, dims, amount, lean):
    listing = rank_table(amount, lean)
    lot = jax.random.randint(jax.random.fold_in(stream_key, 1), dims, 0, int(listing[amount - 1]))
    grade = jnp.searchsorted(jnp.asarray(listing, jnp.int32), lot, side="right")
    return jax.random.permutation(jax.random.fold_in(stream_key, 2), amount)[grade].astype(jnp.int32)


def gaussian(stream_key, dims, spread, limit, shards=(), kind=jnp.bfloat16):
    array = spread * jax.random.normal(stream_key, dims, jnp.float32)
    if shards:
        array = array * levels(stream_key, dims, shards, -0.22, 0.18)
    return jnp.clip(array, -limit, limit).astype(kind)


def setup_inputs(seed: int = 0, part: int = 0) -> dict:
    keys = jax.random.split(jax.random.key(seed), 7)
    part_keys = jax.random.split(jax.random.fold_in(keys[6], part), 7)
    return {
        "activations": gaussian(part_keys[0], (STEPS, ROWS, MODEL_WIDTH), 1.0, 6.0, ((1, 2), (2, 8))),
        "request_adapter_index": touch_ends(skewed_ids(part_keys[1], (STEPS, ROWS), ADAPTER_COUNT, 2), jax.random.fold_in(part_keys[1], 3), 0, ADAPTER_COUNT - 1).astype(jnp.int32),
        "adapter_pool_row": jax.random.permutation(keys[2], ADAPTER_COUNT).astype(jnp.int32),
        "gate_weight_matrix": gaussian(keys[3], (MODEL_WIDTH, HIDDEN_UNITS), MODEL_WIDTH ** -0.5, 0.0625, ((1, 8),)),
        "adapter_down_factors": gaussian(keys[4], (ADAPTER_COUNT, MODEL_WIDTH, ADAPTER_RANK), MODEL_WIDTH ** -0.5, 0.0625, ((0, 2), (1, 8))),
        "adapter_up_factors": gaussian(keys[5], (ADAPTER_COUNT, ADAPTER_RANK, HIDDEN_UNITS), ADAPTER_RANK ** -0.5, 0.75, ((0, 2), (2, 8))),
    }


def reference(activations, request_adapter_index, adapter_pool_row, gate_weight_matrix, adapter_down_factors, adapter_up_factors):
    results = []
    indices = jnp.arange(ADAPTER_COUNT, dtype=jnp.int32)
    for step_index in range(STEPS):
        request_inputs = activations[step_index]
        slots = adapter_pool_row[request_adapter_index[step_index]].astype(jnp.int32)
        base = jnp.dot(request_inputs, gate_weight_matrix, preferred_element_type=jnp.float32)

        def add_shrink(total, position_index):
            lowrank_term = jnp.dot(request_inputs, adapter_down_factors[position_index], preferred_element_type=jnp.float32)
            return total + jnp.where((slots == position_index)[:, None], lowrank_term, jnp.zeros_like(lowrank_term)), None

        shrunk_inputs, _ = lax.scan(add_shrink, jnp.zeros((ROWS, ADAPTER_RANK), jnp.float32), indices)
        shrunk_inputs = shrunk_inputs.astype(jnp.bfloat16)

        def add_delta(total, position_index):
            lowrank_term = jnp.dot(shrunk_inputs, adapter_up_factors[position_index], preferred_element_type=jnp.float32)
            return total + jnp.where((slots == position_index)[:, None], lowrank_term, jnp.zeros_like(lowrank_term)), None

        delta, _ = lax.scan(add_delta, jnp.zeros((ROWS, HIDDEN_UNITS), jnp.float32), indices)
        delta = delta.astype(jnp.bfloat16)
        results.append((base + delta.astype(jnp.float32)).astype(jnp.bfloat16))
    return jnp.stack(results)
```

```python
import jax
import jax.numpy as jnp
from jax import lax
from jax.experimental import pallas as pl
from jax.experimental.pallas import tpu as pltpu
from jax.sharding import PartitionSpec as P

MESH = pl.DeviceIdType.MESH
TILE = 512
LINK_X, LINK_A, LINK_B = 0, 1, 2


def fused_kernel(
    act, slots, down, gate, up, out,
    xg, acc, wbuf, upbuf, downbuf, spread, dsend, drecv, px, pk, rsbuf, agbuf,
    xsend, xrecv, wsem, upsem, insem, pxsem, dsem, rs_send, rs_recv, ag_send, ag_recv, osem,
):
    total = lax.axis_size("tensor")
    me = lax.axis_index("tensor")
    replica = lax.axis_index("replica")
    steps, rows, feats = act.shape
    tiles = out.shape[2] // TILE
    lanes = pk.shape[2]
    rank = lanes // 2
    block = pk.shape[1]
    held = downbuf.shape[0] // rank

    z, x = me // 2, me % 2
    far = z // 2
    zz = z + far * (3 - 2 * z)

    def own_col(k):
        return (k + far * (3 - 2 * k)) * 2 + x

    def other_col(k):
        return (k + far * (3 - 2 * k)) * 2 + 1 - x

    own = [own_col(k) for k in range(4)]
    other = [other_col(k) for k in range(4)]
    corner = [own[0], other[0], own[1], own[2], other[2], own[3], other[1], other[3]]
    middle = [own[1], other[1], own[0], own[2], own[3], other[0], other[2], other[3]]
    order = [zz * m + (1 - zz) * c for c, m in zip(corner, middle)]

    act_copy = pltpu.make_async_copy(act, xg.at[me], insem.at[0])
    act_copy.start()
    down_copy = pltpu.make_async_copy(down, downbuf, insem.at[1])
    down_copy.start()

    mate = z * 2 + 1 - x

    def weights(i):
        start = pl.multiple_of(order[i] * feats, feats)
        return pltpu.make_async_copy(gate.at[pl.ds(start, feats), :], wbuf.at[i % 2], wsem.at[i % 2])

    def up_tile(n):
        cols = pl.ds(pl.multiple_of(n * TILE, TILE), TILE)
        return pltpu.make_async_copy(up.at[:, cols], upbuf.at[n % 2], upsem.at[n % 2])

    weights(0).start()
    up_tile(0).start()

    barrier = pltpu.get_barrier_semaphore()
    for d in range(1, total):
        pl.semaphore_signal(barrier, inc=1, device_id={"tensor": (me + d) % total}, device_id_type=MESH)
    pl.semaphore_signal(barrier, inc=1, device_id={"replica": 1 - replica}, device_id_type=MESH)
    pl.semaphore_wait(barrier, total)

    def piece(slot, half, link, target):
        return pltpu.make_async_remote_copy(
            src_ref=xg.at[slot, half], dst_ref=xg.at[slot, half],
            send_sem=xsend.at[link, slot, half], recv_sem=xrecv.at[slot, half],
            device_id={"tensor": target}, device_id_type=MESH)

    def arrived(slot, half):
        piece(slot, half, LINK_X, mate).wait_recv()

    corner_next = own[1]
    middle_edge, middle_inner = own[0], own[2]
    corner_sends = []
    middle_sends = []

    def corner_send(slot, half, link):
        corner_sends.append((slot, half, link))
        piece(slot, half, link, mate if link == LINK_X else corner_next).start()

    def middle_send(slot, half, link):
        middle_sends.append((slot, half, link))
        piece(slot, half, link, (mate, middle_edge, middle_inner)[link]).start()

    act_copy.wait()
    swap = pltpu.make_async_remote_copy(
        src_ref=xg.at[me], dst_ref=px, send_sem=pxsem.at[0], recv_sem=pxsem.at[1],
        device_id={"replica": 1 - replica}, device_id_type=MESH)
    swap.start()

    @pl.when(zz == 0)
    def _():
        for half in range(2):
            corner_send(own[0], half, LINK_X)
            corner_send(own[0], half, LINK_A)

    @pl.when(zz == 1)
    def _():
        for half in range(2):
            middle_send(own[1], half, LINK_X)
            middle_send(own[1], half, LINK_A)
            middle_send(own[1], half, LINK_B)

    weights(1).start()

    low_lanes = lax.broadcasted_iota(jnp.int32, (rows, lanes), 1) < rank
    lane_half = (lax.broadcasted_iota(jnp.int32, (rows, lanes), 1) >= rank).astype(jnp.int32)

    def partial_shrink(inputs, step, group):
        slot = slots[step, group * rows:(group + 1) * rows, :]
        wanted = jnp.broadcast_to(slot, (rows, lanes)) - lane_half
        found = jnp.zeros((rows, lanes), jnp.float32)
        wide = 2 * lanes
        for t in range(held * rank // wide):
            product = lax.dot_general(
                inputs, downbuf[t * wide:(t + 1) * wide, :], (((1,), (1,)), ((), ())),
                preferred_element_type=jnp.float32)
            for part in range(2):
                first = (t * 2 + part) * 2
                found = found + jnp.where(wanted == first, product[:, part * lanes:(part + 1) * lanes], 0.0)
        return found + pltpu.roll(found, rank, 1)

    down_copy.wait()
    half_blocks = total // 2
    for group in range(2):
        if group == 1:
            swap.wait()
        pair = [
            partial_shrink(px[step] if group else xg[me, step], step, group) for step in range(2)
        ]
        packed = jnp.where(low_lanes, pair[0], pair[1])
        pk[group * half_blocks:(group + 1) * half_blocks] = packed.reshape(half_blocks, block, lanes)

    def reduce_copy(d):
        return pltpu.make_async_remote_copy(
            src_ref=pk.at[(me + d) % total], dst_ref=rsbuf.at[me],
            send_sem=rs_send.at[d], recv_sem=rs_recv.at[d],
            device_id={"tensor": (me + d) % total}, device_id_type=MESH)

    def reduce_arrival(d):
        source = (me + total - d) % total
        return pltpu.make_async_remote_copy(
            src_ref=pk.at[source], dst_ref=rsbuf.at[source],
            send_sem=rs_send.at[d], recv_sem=rs_recv.at[d],
            device_id={"tensor": source}, device_id_type=MESH)

    def gather_copy(d):
        return pltpu.make_async_remote_copy(
            src_ref=agbuf.at[me], dst_ref=agbuf.at[me],
            send_sem=ag_send.at[d], recv_sem=ag_recv.at[d],
            device_id={"tensor": (me + d) % total}, device_id_type=MESH)

    def gather_arrival(d):
        source = (me + total - d) % total
        return pltpu.make_async_remote_copy(
            src_ref=agbuf.at[source], dst_ref=agbuf.at[source],
            send_sem=ag_send.at[d], recv_sem=ag_recv.at[d],
            device_id={"tensor": source}, device_id_type=MESH)

    for d in range(1, total):
        reduce_copy(d).start()

    def multiply(i):
        weights(i).wait()

        def body(n, carry):
            cols = pl.ds(pl.multiple_of(n * TILE, TILE), TILE)
            product = jnp.dot(
                xg[order[i]].reshape(steps * rows, feats), wbuf[i % 2, :, cols],
                preferred_element_type=jnp.float32)
            if i == 0:
                acc[n] = product
            else:
                acc[n] += product
            return carry

        lax.fori_loop(0, tiles, body, 0)
        if i + 2 < total:
            weights(i + 2).start()

    multiply(0)

    for d in range(1, total):
        reduce_arrival(d).wait_recv()
    summed = pk[me]
    for d in range(1, total):
        summed = summed + rsbuf[(me + total - d) % total]
    agbuf[me] = summed.astype(jnp.bfloat16)
    for d in range(1, total):
        gather_copy(d).start()

    @pl.when(zz == 0)
    def _():
        arrived(own[1], 0)
        corner_send(own[1], 0, LINK_X)

    @pl.when(zz == 1)
    def _():
        arrived(own[2], 0)
        middle_send(own[2], 0, LINK_A)
        middle_send(own[2], 0, LINK_X)
        arrived(own[0], 0)
        middle_send(own[0], 0, LINK_X)
        middle_send(own[0], 0, LINK_B)

    for d in range(1, total):
        gather_arrival(d).wait_recv()

    def fill_spread(group):
        packed = agbuf[group * half_blocks:(group + 1) * half_blocks].reshape(rows, lanes).astype(jnp.float32)
        turned = pltpu.roll(packed, rank, 1)
        for step in range(2):
            both = jnp.where(low_lanes, packed, turned) if step == 0 else jnp.where(low_lanes, turned, packed)
            slot = slots[step, group * rows:(group + 1) * rows, :]
            wanted = jnp.broadcast_to(slot, (rows, lanes)) - lane_half
            for t in range(held // 2):
                spread[step * rows:(step + 1) * rows, t * lanes:(t + 1) * lanes] = jnp.where(
                    wanted == 2 * t, both, 0.0).astype(jnp.bfloat16)

    def expand(group):
        fill_spread(group)

        def body(n, carry):
            up_tile(n).wait()

            @pl.when(n + 1 < tiles)
            def _():
                up_tile(n + 1).start()

            delta = jnp.dot(spread[...], upbuf[n % 2], preferred_element_type=jnp.float32)
            if group == 1:
                dsend[n] = delta.astype(jnp.bfloat16)
            else:
                acc[n] += delta
            return carry

        lax.fori_loop(0, tiles, body, 0)

    expand(1)
    back = pltpu.make_async_remote_copy(
        src_ref=dsend, dst_ref=drecv, send_sem=dsem.at[0], recv_sem=dsem.at[1],
        device_id={"replica": 1 - replica}, device_id_type=MESH)
    back.start()
    up_tile(0).start()

    @pl.when(zz == 0)
    def _():
        arrived(other[0], 1)
        corner_send(other[0], 1, LINK_A)

    @pl.when(zz == 1)
    def _():
        arrived(own[2], 1)
        middle_send(own[2], 1, LINK_A)
        arrived(own[0], 1)
        middle_send(own[0], 1, LINK_B)
        arrived(other[1], 1)
        middle_send(other[1], 1, LINK_B)

    arrived(order[1], 0)
    multiply(1)

    @pl.when(zz == 0)
    def _():
        arrived(own[1], 1)

    multiply(2)

    @pl.when(zz == 0)
    def _():
        arrived(own[2], 0)
        corner_send(own[2], 0, LINK_X)

    @pl.when(zz == 1)
    def _():
        arrived(own[3], 0)
        middle_send(own[3], 0, LINK_A)
        middle_send(own[3], 0, LINK_X)

    expand(0)

    @pl.when(zz == 0)
    def _():
        arrived(own[2], 1)
        corner_send(own[2], 1, LINK_X)

    @pl.when(zz == 1)
    def _():
        arrived(own[3], 1)
        middle_send(own[3], 1, LINK_A)
        middle_send(own[3], 1, LINK_X)
        middle_send(other[1], 1, LINK_A)

    multiply(3)

    @pl.when(zz == 0)
    def _():
        arrived(own[3], 0)
        corner_send(own[3], 0, LINK_X)
        arrived(other[2], 0)
        arrived(other[2], 1)

    multiply(4)

    @pl.when(zz == 0)
    def _():
        arrived(own[3], 1)
        corner_send(own[3], 1, LINK_X)

    @pl.when(zz == 1)
    def _():
        arrived(other[0], 0)
        arrived(other[0], 1)

    multiply(5)
    arrived(order[6], 0)
    arrived(order[6], 1)
    multiply(6)
    back.wait()
    arrived(order[7], 0)
    arrived(order[7], 1)

    weights(7).wait()

    def result(n, step):
        cols = pl.ds(pl.multiple_of(n * TILE, TILE), TILE)
        return pltpu.make_async_copy(
            dsend.at[n, pl.ds(step * rows, rows), :], out.at[step, :, cols], osem.at[n, step])

    def finish(n, carry):
        cols = pl.ds(pl.multiple_of(n * TILE, TILE), TILE)
        product = jnp.dot(
            xg[order[7]].reshape(steps * rows, feats), wbuf[1, :, cols],
            preferred_element_type=jnp.float32)
        dsend[n] = (acc[n] + product + drecv[n].astype(jnp.float32)).astype(jnp.bfloat16)
        for step in range(2):
            result(n, step).start()
        return carry

    lax.fori_loop(0, tiles, finish, 0)

    @pl.when(zz == 0)
    def _():
        for slot, half, link in corner_sends:
            piece(slot, half, link, mate).wait_send()

    @pl.when(zz == 1)
    def _():
        for slot, half, link in middle_sends:
            piece(slot, half, link, mate).wait_send()

    for d in range(1, total):
        reduce_copy(d).wait_send()
        gather_copy(d).wait_send()
    for n in range(tiles):
        for step in range(2):
            result(n, step).wait()


def fused(activations, slots, down, gate, up):
    steps, rows, feats = activations.shape
    total = lax.axis_size("tensor")
    columns = gate.shape[1]
    tiles = columns // TILE
    rank = up.shape[1]
    held = up.shape[0]
    wide = held * rank
    flops = 2 * steps * rows * columns * (feats * total + 2 * wide)
    return pl.pallas_call(
        fused_kernel,
        out_shape=jax.ShapeDtypeStruct((steps, rows, columns), jnp.bfloat16),
        in_specs=[
            pl.BlockSpec(memory_space=pl.ANY),
            pl.BlockSpec(memory_space=pltpu.VMEM),
            pl.BlockSpec(memory_space=pl.ANY),
            pl.BlockSpec(memory_space=pl.ANY),
            pl.BlockSpec(memory_space=pl.ANY),
        ],
        out_specs=pl.BlockSpec(memory_space=pl.ANY),
        scratch_shapes=[
            pltpu.VMEM((total, steps, rows, feats), jnp.bfloat16),
            pltpu.VMEM((tiles, steps * rows, TILE), jnp.float32),
            pltpu.VMEM((2, feats, columns), jnp.bfloat16),
            pltpu.VMEM((2, wide, TILE), jnp.bfloat16),
            pltpu.VMEM((wide, feats), jnp.bfloat16),
            pltpu.VMEM((steps * rows, wide), jnp.bfloat16),
            pltpu.VMEM((tiles, steps * rows, TILE), jnp.bfloat16),
            pltpu.VMEM((tiles, steps * rows, TILE), jnp.bfloat16),
            pltpu.VMEM((steps, rows, feats), jnp.bfloat16),
            pltpu.VMEM((total, 2 * rows // total, 2 * rank), jnp.float32),
            pltpu.VMEM((total, 2 * rows // total, 2 * rank), jnp.float32),
            pltpu.VMEM((total, 2 * rows // total, 2 * rank), jnp.bfloat16),
            pltpu.SemaphoreType.DMA((3, total, 2)),
            pltpu.SemaphoreType.DMA((total, 2)),
            pltpu.SemaphoreType.DMA((2,)),
            pltpu.SemaphoreType.DMA((2,)),
            pltpu.SemaphoreType.DMA((2,)),
            pltpu.SemaphoreType.DMA((2,)),
            pltpu.SemaphoreType.DMA((2,)),
            pltpu.SemaphoreType.DMA((total,)),
            pltpu.SemaphoreType.DMA((total,)),
            pltpu.SemaphoreType.DMA((total,)),
            pltpu.SemaphoreType.DMA((total,)),
            pltpu.SemaphoreType.DMA((tiles, 2)),
        ],
        compiler_params=pltpu.CompilerParams(
            collective_id=0, has_side_effects=True, vmem_limit_bytes=60 * 1024 * 1024),
        cost_estimate=pl.CostEstimate(flops=flops, bytes_accessed=80 * 1024 * 1024, transcendentals=0),
    )(
        activations, slots,
        jnp.swapaxes(down, 1, 2).reshape(wide, feats), gate, up.reshape(wide, columns))


def on_device_fused(
    activations, request_adapter_index, adapter_pool_row, gate_weight_matrix, adapter_down_factors, adapter_up_factors
):
    replica_index = lax.axis_index("replica")
    rows_dev = activations.shape[1]
    held = adapter_down_factors.shape[0]
    table = jnp.arange(adapter_pool_row.shape[0], dtype=jnp.int32)
    matches = request_adapter_index[:, :, None] == table
    slots = jnp.sum(jnp.where(matches, adapter_pool_row, 0), axis=2, keepdims=True) - replica_index * held
    turned = jnp.concatenate([slots[:, rows_dev:], slots[:, :rows_dev]], axis=1)
    slots = jnp.where(replica_index == 0, slots, turned)
    return fused(activations, slots, adapter_down_factors, gate_weight_matrix, adapter_up_factors)


def swapped(value, axis, bit):
    return lax.ppermute(value, axis, [(i, i ^ 1 << bit) for i in range(lax.axis_size(axis))])


def pool_rows(row_ids, adapter_pool_row):
    table = jnp.arange(adapter_pool_row.shape[0], dtype=jnp.int32)
    matches = row_ids[:, None] == table[None, :]
    return jnp.sum(jnp.where(matches, adapter_pool_row[None, :], 0), axis=1)


def adapter_delta(row_inputs, local_slots, down_pool, up_pool):
    held = down_pool.shape[0]
    owned = local_slots[:, None] == jnp.arange(held, dtype=jnp.int32)[None, :]
    partial_all = jnp.einsum(
        "nd,adr->nar", row_inputs, down_pool, preferred_element_type=jnp.float32
    )
    partial_value = jnp.sum(jnp.where(owned[:, :, None], partial_all, 0.0), axis=1)
    shrunk_inputs = lax.psum(partial_value, "tensor").astype(jnp.bfloat16)
    spread = jnp.where(
        owned[:, :, None], shrunk_inputs[:, None, :], jnp.zeros_like(shrunk_inputs)[:, None, :]
    )
    spread = spread.reshape(spread.shape[0], held * spread.shape[2])
    flat_up = up_pool.reshape(held * up_pool.shape[1], up_pool.shape[2])
    return jnp.dot(spread, flat_up, preferred_element_type=jnp.float32).astype(jnp.bfloat16)


def on_device(
    activations,
    request_adapter_index,
    adapter_pool_row,
    gate_weight_matrix,
    adapter_down_factors,
    adapter_up_factors,
):
    replica_index = lax.axis_index("replica")
    rows_dev = activations.shape[1]
    held = adapter_down_factors.shape[0]
    own_ids = lax.dynamic_slice_in_dim(request_adapter_index, replica_index * rows_dev, rows_dev, 1)
    other_ids = lax.dynamic_slice_in_dim(
        request_adapter_index, (1 - replica_index) * rows_dev, rows_dev, 1
    )
    partner_inputs = swapped(activations, "replica", 0)
    steps_total = activations.shape[0]
    results = []
    for step_index in range(steps_total):
        own_inputs = activations[step_index]
        base = jnp.dot(
            lax.all_gather(own_inputs, "tensor", axis=1, tiled=True),
            gate_weight_matrix,
            preferred_element_type=jnp.float32,
        )
        own_slots = pool_rows(own_ids[step_index], adapter_pool_row)
        count = own_inputs.shape[0]
        both_inputs = jnp.concatenate([own_inputs, partner_inputs[step_index]], axis=0)
        both_slots = (
            jnp.concatenate([own_slots, pool_rows(other_ids[step_index], adapter_pool_row)], axis=0)
            - replica_index * held
        )
        both_delta = adapter_delta(
            both_inputs, both_slots, adapter_down_factors, adapter_up_factors
        )
        returned = swapped(both_delta[count:], "replica", 0)
        delta = both_delta[:count].astype(jnp.float32) + returned.astype(jnp.float32)
        results.append((base + delta).astype(jnp.bfloat16))
    return jnp.stack(results)


def solution(mesh):
    fits = mesh.shape["tensor"] == 8 and mesh.shape["replica"] == 2
    return jax.shard_map(
        on_device_fused if fits else on_device,
        mesh=mesh,
        in_specs=(
            P(None, ("groups", "replica"), "tensor"),
            P(None, "groups"),
            P(),
            P(None, "tensor"),
            P("replica", "tensor", None),
            P("replica", None, "tensor"),
        ),
        out_specs=P(None, ("groups", "replica"), "tensor"),
        check_vma=False,
    )
```

```python
import jax
import jax.numpy as jnp
from jax import lax
from jax.experimental import pallas as pl
from jax.experimental.pallas import tpu as pltpu
from jax.sharding import PartitionSpec as P

MESH = pl.DeviceIdType.MESH
TILE = 896
LINK_X, LINK_A, LINK_B = 0, 1, 2


def fused_kernel(
    act, slots, down, gate, up, out,
    xg, acc, wbuf, upbuf, downbuf, spread, dsend, drecv, px, pk, rsbuf, agbuf,
    xsend, xrecv, wsem, upsem, insem, pxsem, dsem, rs_send, rs_recv, ag_send, ag_recv, osem,
):
    total = lax.axis_size("tensor")
    me = lax.axis_index("tensor")
    replica = lax.axis_index("replica")
    steps, rows, feats = act.shape
    tiles = out.shape[2] // TILE
    lanes = pk.shape[2]
    rank = lanes // 2
    block = pk.shape[1]
    held = downbuf.shape[0] // rank

    z, x = me // 2, me % 2
    far = z // 2
    zz = z + far * (3 - 2 * z)

    def own_col(k):
        return (k + far * (3 - 2 * k)) * 2 + x

    def other_col(k):
        return (k + far * (3 - 2 * k)) * 2 + 1 - x

    own = [own_col(k) for k in range(4)]
    other = [other_col(k) for k in range(4)]
    corner = [own[0], other[0], own[1], own[2], other[2], own[3], other[1], other[3]]
    middle = [own[1], other[1], own[0], own[2], own[3], other[0], other[2], other[3]]
    order = [zz * m + (1 - zz) * c for c, m in zip(corner, middle)]

    act_copy = pltpu.make_async_copy(act, xg.at[me], insem.at[0])
    act_copy.start()
    down_copy = pltpu.make_async_copy(down, downbuf, insem.at[1])
    down_copy.start()

    mate = z * 2 + 1 - x

    def weights(i):
        start = pl.multiple_of(order[i] * feats, feats)
        return pltpu.make_async_copy(gate.at[pl.ds(start, feats), :], wbuf.at[i % 2], wsem.at[i % 2])

    def up_tile(n):
        cols = pl.ds(pl.multiple_of(n * TILE, TILE), TILE)
        return pltpu.make_async_copy(up.at[:, cols], upbuf.at[n % 2], upsem.at[n % 2])

    weights(0).start()
    up_tile(0).start()

    barrier = pltpu.get_barrier_semaphore()
    for d in range(1, total):
        pl.semaphore_signal(barrier, inc=1, device_id={"tensor": (me + d) % total}, device_id_type=MESH)
    pl.semaphore_signal(barrier, inc=1, device_id={"replica": 1 - replica}, device_id_type=MESH)
    pl.semaphore_wait(barrier, total)

    def piece(slot, half, link, target):
        return pltpu.make_async_remote_copy(
            src_ref=xg.at[slot, half], dst_ref=xg.at[slot, half],
            send_sem=xsend.at[link, slot, half], recv_sem=xrecv.at[slot, half],
            device_id={"tensor": target}, device_id_type=MESH)

    def arrived(slot, half):
        piece(slot, half, LINK_X, mate).wait_recv()

    corner_next = own[1]
    middle_edge, middle_inner = own[0], own[2]
    corner_sends = []
    middle_sends = []

    def corner_send(slot, half, link):
        corner_sends.append((slot, half, link))
        piece(slot, half, link, mate if link == LINK_X else corner_next).start()

    def middle_send(slot, half, link):
        middle_sends.append((slot, half, link))
        piece(slot, half, link, (mate, middle_edge, middle_inner)[link]).start()

    act_copy.wait()
    swap = pltpu.make_async_remote_copy(
        src_ref=xg.at[me], dst_ref=px, send_sem=pxsem.at[0], recv_sem=pxsem.at[1],
        device_id={"replica": 1 - replica}, device_id_type=MESH)
    swap.start()

    def send_own(half):
        @pl.when(zz == 0)
        def _():
            corner_send(own[0], half, LINK_X)
            corner_send(own[0], half, LINK_A)

        @pl.when(zz == 1)
        def _():
            middle_send(own[1], half, LINK_A)
            middle_send(own[1], half, LINK_X)
            middle_send(own[1], half, LINK_B)

    send_own(0)
    weights(1).start()

    both_rows = steps * rows
    half_blocks = total // 2
    low_lanes = lax.broadcasted_iota(jnp.int32, (rows, lanes), 1) < rank
    lane_half = (lax.broadcasted_iota(jnp.int32, (both_rows, lanes), 1) >= rank).astype(jnp.int32)

    def wanted_first(group):
        slot = slots[:, group * rows:(group + 1) * rows, :].reshape(both_rows, 1)
        return jnp.broadcast_to(slot, (both_rows, lanes)) - lane_half

    def partial_shrink(inputs, group):
        wanted = wanted_first(group)
        found = jnp.zeros((both_rows, lanes), jnp.float32)
        wide = 2 * lanes
        for t in range(held * rank // wide):
            product = lax.dot_general(
                inputs, downbuf[t * wide:(t + 1) * wide, :], (((1,), (1,)), ((), ())),
                preferred_element_type=jnp.float32)
            for part in range(2):
                first = (t * 2 + part) * 2
                found = found + jnp.where(wanted == first, product[:, part * lanes:(part + 1) * lanes], 0.0)
        both = found + pltpu.roll(found, rank, 1)
        packed = jnp.where(low_lanes, both[:rows], both[rows:])
        pk[group * half_blocks:(group + 1) * half_blocks] = packed.reshape(
            half_blocks, block, lanes).astype(jnp.bfloat16)

    down_copy.wait()
    partial_shrink(xg[me].reshape(both_rows, feats), 0)
    swap.wait()
    partial_shrink(px[...].reshape(both_rows, feats), 1)

    def reduce_copy(d):
        return pltpu.make_async_remote_copy(
            src_ref=pk.at[(me + d) % total], dst_ref=rsbuf.at[me],
            send_sem=rs_send.at[d], recv_sem=rs_recv.at[d],
            device_id={"tensor": (me + d) % total}, device_id_type=MESH)

    def reduce_arrival(d):
        source = (me + total - d) % total
        return pltpu.make_async_remote_copy(
            src_ref=pk.at[source], dst_ref=rsbuf.at[source],
            send_sem=rs_send.at[d], recv_sem=rs_recv.at[d],
            device_id={"tensor": source}, device_id_type=MESH)

    def gather_copy(d):
        return pltpu.make_async_remote_copy(
            src_ref=agbuf.at[me], dst_ref=agbuf.at[me],
            send_sem=ag_send.at[d], recv_sem=ag_recv.at[d],
            device_id={"tensor": (me + d) % total}, device_id_type=MESH)

    def gather_arrival(d):
        source = (me + total - d) % total
        return pltpu.make_async_remote_copy(
            src_ref=agbuf.at[source], dst_ref=agbuf.at[source],
            send_sem=ag_send.at[d], recv_sem=ag_recv.at[d],
            device_id={"tensor": source}, device_id_type=MESH)

    for d in range(1, total):
        reduce_copy(d).start()
    send_own(1)

    def multiply(i):
        weights(i).wait()

        def body(n, carry):
            cols = pl.ds(pl.multiple_of(n * TILE, TILE), TILE)
            product = jnp.dot(
                xg[order[i]].reshape(steps * rows, feats), wbuf[i % 2, :, cols],
                preferred_element_type=jnp.float32)
            if i == 0:
                acc[n] = product
            else:
                acc[n] += product
            return carry

        lax.fori_loop(0, tiles, body, 0)
        if i + 2 < total:
            weights(i + 2).start()

    multiply(0)

    @pl.when(zz == 0)
    def _():
        arrived(own[1], 0)
        corner_send(own[1], 0, LINK_X)

    @pl.when(zz == 1)
    def _():
        arrived(own[2], 0)
        middle_send(own[2], 0, LINK_A)
        middle_send(own[2], 0, LINK_X)
        arrived(own[0], 0)
        middle_send(own[0], 0, LINK_X)
        middle_send(own[0], 0, LINK_B)

    for d in range(1, total):
        reduce_arrival(d).wait_recv()
    summed = pk[me].astype(jnp.float32)
    for d in range(1, total):
        summed = summed + rsbuf[(me + total - d) % total].astype(jnp.float32)
    agbuf[me] = summed.astype(jnp.bfloat16)
    for d in range(1, total):
        gather_copy(d).start()

    def fill_spread(group):
        packed = agbuf[group * half_blocks:(group + 1) * half_blocks].reshape(rows, lanes).astype(jnp.float32)
        turned = pltpu.roll(packed, rank, 1)
        both = jnp.concatenate(
            [jnp.where(low_lanes, packed, turned), jnp.where(low_lanes, turned, packed)], axis=0)
        wanted = wanted_first(group)
        for t in range(held // 2):
            spread[:, t * lanes:(t + 1) * lanes] = jnp.where(wanted == 2 * t, both, 0.0).astype(jnp.bfloat16)

    def expand(group):
        fill_spread(group)

        def body(n, carry):
            up_tile(n).wait()

            @pl.when(n + 1 < tiles)
            def _():
                up_tile(n + 1).start()

            delta = jnp.dot(spread[...], upbuf[n % 2], preferred_element_type=jnp.float32)
            if group == 1:
                dsend[n] = delta.astype(jnp.bfloat16)
            else:
                acc[n] += delta
            return carry

        lax.fori_loop(0, tiles, body, 0)

    @pl.when(zz == 0)
    def _():
        arrived(other[0], 1)
        corner_send(other[0], 1, LINK_A)

    @pl.when(zz == 1)
    def _():
        arrived(own[2], 1)
        middle_send(own[2], 1, LINK_A)
        arrived(own[0], 1)
        middle_send(own[0], 1, LINK_B)
        arrived(other[1], 1)
        middle_send(other[1], 1, LINK_B)

    arrived(order[1], 0)
    multiply(1)

    @pl.when(zz == 0)
    def _():
        arrived(own[1], 1)

    multiply(2)

    @pl.when(zz == 0)
    def _():
        arrived(own[2], 0)
        corner_send(own[2], 0, LINK_X)

    @pl.when(zz == 1)
    def _():
        arrived(own[3], 0)
        middle_send(own[3], 0, LINK_A)
        middle_send(own[3], 0, LINK_X)

    for d in range(1, total):
        gather_arrival(d).wait_recv()

    expand(1)
    back = pltpu.make_async_remote_copy(
        src_ref=dsend, dst_ref=drecv, send_sem=dsem.at[0], recv_sem=dsem.at[1],
        device_id={"replica": 1 - replica}, device_id_type=MESH)
    back.start()
    up_tile(0).start()

    @pl.when(zz == 0)
    def _():
        arrived(own[2], 1)
        corner_send(own[2], 1, LINK_X)

    @pl.when(zz == 1)
    def _():
        arrived(own[3], 1)
        middle_send(own[3], 1, LINK_A)
        middle_send(own[3], 1, LINK_X)
        middle_send(other[1], 1, LINK_A)

    expand(0)

    multiply(3)

    @pl.when(zz == 0)
    def _():
        arrived(own[3], 0)
        corner_send(own[3], 0, LINK_X)
        arrived(other[2], 0)
        arrived(other[2], 1)

    multiply(4)

    @pl.when(zz == 0)
    def _():
        arrived(own[3], 1)
        corner_send(own[3], 1, LINK_X)

    @pl.when(zz == 1)
    def _():
        arrived(other[0], 0)
        arrived(other[0], 1)

    multiply(5)
    def multiply_half(i, half):
        part = pl.ds(half * rows, rows)

        def body(n, carry):
            cols = pl.ds(pl.multiple_of(n * TILE, TILE), TILE)
            acc[n, part] += jnp.dot(
                xg[order[i], half], wbuf[i % 2, :, cols], preferred_element_type=jnp.float32)
            return carry

        lax.fori_loop(0, tiles, body, 0)

    def result(n, step):
        cols = pl.ds(pl.multiple_of(n * TILE, TILE), TILE)
        return pltpu.make_async_copy(
            dsend.at[n, pl.ds(step * rows, rows), :], out.at[step, :, cols], osem.at[n, step])

    def finish(i, step):
        part = pl.ds(step * rows, rows)

        def body(n, carry):
            cols = pl.ds(pl.multiple_of(n * TILE, TILE), TILE)
            product = jnp.dot(
                xg[order[i], step], wbuf[i % 2, :, cols], preferred_element_type=jnp.float32)
            dsend[n, part] = (acc[n, part] + product + drecv[n, part].astype(jnp.float32)).astype(jnp.bfloat16)
            result(n, step).start()
            return carry

        lax.fori_loop(0, tiles, body, 0)

    arrived(order[6], 0)
    weights(6).wait()
    multiply_half(6, 0)
    back.wait()
    arrived(order[7], 0)
    weights(7).wait()
    finish(7, 0)
    arrived(order[6], 1)
    multiply_half(6, 1)
    arrived(order[7], 1)
    finish(7, 1)

    @pl.when(zz == 0)
    def _():
        for slot, half, link in corner_sends:
            piece(slot, half, link, mate).wait_send()

    @pl.when(zz == 1)
    def _():
        for slot, half, link in middle_sends:
            piece(slot, half, link, mate).wait_send()

    for d in range(1, total):
        reduce_copy(d).wait_send()
        gather_copy(d).wait_send()
    for n in range(tiles):
        for step in range(2):
            result(n, step).wait()


def fused(activations, slots, down, gate, up):
    steps, rows, feats = activations.shape
    total = lax.axis_size("tensor")
    columns = gate.shape[1]
    tiles = columns // TILE
    rank = up.shape[1]
    held = up.shape[0]
    wide = held * rank
    flops = 2 * steps * rows * columns * (feats * total + 2 * wide)
    return pl.pallas_call(
        fused_kernel,
        out_shape=jax.ShapeDtypeStruct((steps, rows, columns), jnp.bfloat16),
        in_specs=[
            pl.BlockSpec(memory_space=pl.ANY),
            pl.BlockSpec(memory_space=pltpu.VMEM),
            pl.BlockSpec(memory_space=pl.ANY),
            pl.BlockSpec(memory_space=pl.ANY),
            pl.BlockSpec(memory_space=pl.ANY),
        ],
        out_specs=pl.BlockSpec(memory_space=pl.ANY),
        scratch_shapes=[
            pltpu.VMEM((total, steps, rows, feats), jnp.bfloat16),
            pltpu.VMEM((tiles, steps * rows, TILE), jnp.float32),
            pltpu.VMEM((2, feats, columns), jnp.bfloat16),
            pltpu.VMEM((2, wide, TILE), jnp.bfloat16),
            pltpu.VMEM((wide, feats), jnp.bfloat16),
            pltpu.VMEM((steps * rows, wide), jnp.bfloat16),
            pltpu.VMEM((tiles, steps * rows, TILE), jnp.bfloat16),
            pltpu.VMEM((tiles, steps * rows, TILE), jnp.bfloat16),
            pltpu.VMEM((steps, rows, feats), jnp.bfloat16),
            pltpu.VMEM((total, 2 * rows // total, 2 * rank), jnp.bfloat16),
            pltpu.VMEM((total, 2 * rows // total, 2 * rank), jnp.bfloat16),
            pltpu.VMEM((total, 2 * rows // total, 2 * rank), jnp.bfloat16),
            pltpu.SemaphoreType.DMA((3, total, 2)),
            pltpu.SemaphoreType.DMA((total, 2)),
            pltpu.SemaphoreType.DMA((2,)),
            pltpu.SemaphoreType.DMA((2,)),
            pltpu.SemaphoreType.DMA((2,)),
            pltpu.SemaphoreType.DMA((2,)),
            pltpu.SemaphoreType.DMA((2,)),
            pltpu.SemaphoreType.DMA((total,)),
            pltpu.SemaphoreType.DMA((total,)),
            pltpu.SemaphoreType.DMA((total,)),
            pltpu.SemaphoreType.DMA((total,)),
            pltpu.SemaphoreType.DMA((tiles, 2)),
        ],
        compiler_params=pltpu.CompilerParams(
            collective_id=0, has_side_effects=True, vmem_limit_bytes=60 * 1024 * 1024),
        cost_estimate=pl.CostEstimate(flops=flops, bytes_accessed=80 * 1024 * 1024, transcendentals=0),
    )(
        activations, slots,
        jnp.swapaxes(down, 1, 2).reshape(wide, feats), gate, up.reshape(wide, columns))


def on_device_fused(
    activations, request_adapter_index, adapter_pool_row, gate_weight_matrix, adapter_down_factors, adapter_up_factors
):
    replica_index = lax.axis_index("replica")
    rows_dev = activations.shape[1]
    held = adapter_down_factors.shape[0]
    table = jnp.arange(adapter_pool_row.shape[0], dtype=jnp.int32)
    matches = request_adapter_index[:, :, None] == table
    slots = jnp.sum(jnp.where(matches, adapter_pool_row, 0), axis=2, keepdims=True) - replica_index * held
    turned = jnp.concatenate([slots[:, rows_dev:], slots[:, :rows_dev]], axis=1)
    slots = jnp.where(replica_index == 0, slots, turned)
    return fused(activations, slots, adapter_down_factors, gate_weight_matrix, adapter_up_factors)


def swapped(value, axis, bit):
    return lax.ppermute(value, axis, [(i, i ^ 1 << bit) for i in range(lax.axis_size(axis))])


def pool_rows(row_ids, adapter_pool_row):
    table = jnp.arange(adapter_pool_row.shape[0], dtype=jnp.int32)
    matches = row_ids[:, None] == table[None, :]
    return jnp.sum(jnp.where(matches, adapter_pool_row[None, :], 0), axis=1)


def adapter_delta(row_inputs, local_slots, down_pool, up_pool):
    held = down_pool.shape[0]
    owned = local_slots[:, None] == jnp.arange(held, dtype=jnp.int32)[None, :]
    partial_all = jnp.einsum(
        "nd,adr->nar", row_inputs, down_pool, preferred_element_type=jnp.float32
    )
    partial_value = jnp.sum(jnp.where(owned[:, :, None], partial_all, 0.0), axis=1)
    shrunk_inputs = lax.psum(partial_value, "tensor").astype(jnp.bfloat16)
    spread = jnp.where(
        owned[:, :, None], shrunk_inputs[:, None, :], jnp.zeros_like(shrunk_inputs)[:, None, :]
    )
    spread = spread.reshape(spread.shape[0], held * spread.shape[2])
    flat_up = up_pool.reshape(held * up_pool.shape[1], up_pool.shape[2])
    return jnp.dot(spread, flat_up, preferred_element_type=jnp.float32).astype(jnp.bfloat16)


def on_device(
    activations,
    request_adapter_index,
    adapter_pool_row,
    gate_weight_matrix,
    adapter_down_factors,
    adapter_up_factors,
):
    replica_index = lax.axis_index("replica")
    rows_dev = activations.shape[1]
    held = adapter_down_factors.shape[0]
    own_ids = lax.dynamic_slice_in_dim(request_adapter_index, replica_index * rows_dev, rows_dev, 1)
    other_ids = lax.dynamic_slice_in_dim(
        request_adapter_index, (1 - replica_index) * rows_dev, rows_dev, 1
    )
    partner_inputs = swapped(activations, "replica", 0)
    steps_total = activations.shape[0]
    results = []
    for step_index in range(steps_total):
        own_inputs = activations[step_index]
        base = jnp.dot(
            lax.all_gather(own_inputs, "tensor", axis=1, tiled=True),
            gate_weight_matrix,
            preferred_element_type=jnp.float32,
        )
        own_slots = pool_rows(own_ids[step_index], adapter_pool_row)
        count = own_inputs.shape[0]
        both_inputs = jnp.concatenate([own_inputs, partner_inputs[step_index]], axis=0)
        both_slots = (
            jnp.concatenate([own_slots, pool_rows(other_ids[step_index], adapter_pool_row)], axis=0)
            - replica_index * held
        )
        both_delta = adapter_delta(
            both_inputs, both_slots, adapter_down_factors, adapter_up_factors
        )
        returned = swapped(both_delta[count:], "replica", 0)
        delta = both_delta[:count].astype(jnp.float32) + returned.astype(jnp.float32)
        results.append((base + delta).astype(jnp.bfloat16))
    return jnp.stack(results)


def solution(mesh):
    fits = mesh.shape["tensor"] == 8 and mesh.shape["replica"] == 2
    return jax.shard_map(
        on_device_fused if fits else on_device,
        mesh=mesh,
        in_specs=(
            P(None, ("groups", "replica"), "tensor"),
            P(None, "groups"),
            P(),
            P(None, "tensor"),
            P("replica", "tensor", None),
            P("replica", None, "tensor"),
        ),
        out_specs=P(None, ("groups", "replica"), "tensor"),
        check_vma=False,
    )
```
